256 devices in a mesh: section: 8 (over z_hi, x), expert: 32 (over z_lo, y, core).
Axes of the slice: x: 4, y: 4, z: 8 (z_hi: 2, z_lo: 4; z = z_hi * 4 + z_lo), core: 2. Of those that a mesh axis runs over, the one named last changes fastest.
Arguments:
- forward_acts: bfloat16 [8, 4096, 2048], P('section', 'expert'), may hold values from -6 to 6
- forward_routes: int32 [8, 4096, 2], P('section', 'expert'), may hold values from 0 to 31, all different within a row; in each aligned block of 128 rows (0 to 127, 128 to 255, ..., all dimensions but the last counted through in order) at most 16 rows name the same one
- forward_gates: float32 [8, 4096, 2], P('section', 'expert'), may hold values from 0 to 1, as said below
- weight_in: bfloat16 [8, 32, 2048, 1536], P('section', 'expert'), may hold values from -0.125 to 0.125
- weight_down: bfloat16 [8, 32, 768, 2048], P('section', 'expert'), may hold values from -0.21875 to 0.21875
- saved_acts: bfloat16 [8, 4096, 2048], P('section', 'expert'), may hold values from -6 to 6
- backward_routes: int32 [8, 4096, 2], P('section', 'expert'), may hold values from 0 to 31, all different within a row; in each aligned block of 128 rows (0 to 127, 128 to 255, ..., all dimensions but the last counted through in order) at most 16 rows name the same one
- backward_gates: float32 [8, 4096, 2], P('section', 'expert'), may hold values from 0 to 1, as said below
- sent_grads: bfloat16 [8, 4096, 2048], P('section', 'expert'), may hold values from -6 to 6
Outputs:
- layer_out: bfloat16 [8, 4096, 2048], P('section', 'expert')
- input_grads: bfloat16 [8, 4096, 2048], P('section', 'expert')
The draws below stay inside these ranges and needn't reach their ends.
Inputs may be any that keep to these rules, and one draw needn't show every extreme that they name: `forward_routes`: each row names 2 different experts. Among the entries of one section's tokens of one device (aligned blocks of 128 tokens) no expert is named more than 16 times, a bound that some block reaches. `backward_routes`: each row names 2 different experts. Among the entries of one section's tokens of one device (aligned blocks of 128 tokens) no expert is named more than 16 times, a bound that some block reaches. `forward_gates`: each row is positive and sums to 1. `backward_gates`: each row is positive and sums to 1.
All inputs are finite; a program needn't handle non-finite values.
Results may differ from the reference program's by a relative error of at most 0.008.
Values may be sent and summed in bfloat16 or wider, within the bound.
A program may use at most 64 MiB of HBM per device.

```python
import math
import jax
import jax.numpy as jnp
import numpy as np
from jax import lax

D = 2048
FF = 768
TOPK = 2
TOK_DEV = 128
SECTIONS = 8
EXPERTS = 32
TOKENS = 4096
CAP = 16


def gate_values(key, spread):
    logits = spread * jax.random.normal(key, (SECTIONS, TOKENS, TOPK), jnp.float32)
    return jax.nn.softmax(logits, axis=-1)


def draw_forward_gates(key, part):
    key = jax.random.fold_in(key, 11)
    return gate_values(key, 1.5)


def draw_backward_gates(key, part):
    key = jax.random.fold_in(key, 23)
    return gate_values(key, 1.5)


def levels(own_key, dims, split, smallest, top_value):
    loudness = 1.0
    for position, shards_of in split:
        draws = jax.random.uniform(jax.random.fold_in(jax.random.fold_in(own_key, 6), position), (shards_of,), jnp.float32, smallest / len(split), top_value / len(split))
        loudness = loudness * jnp.repeat(jnp.exp(draws), dims[position] // shards_of).reshape((-1,) + (1,) * (len(dims) - 1 - position))
    return loudness


def shared_out(rng, own, number, rows, number_of, top, reach, lean):
    sequence = jax.random.permutation(rng, number_of)
    crowded, common = load_shares(number_of, rows * top, reach, lean, True), load_shares(number_of, rows * top, reach, lean, False)
    places = jnp.arange(number_of)

    def named(sizes, offset_by):
        used = int((sizes > 0).sum())
        fixed = max(1, used // 4)
        moved = fixed + (places - fixed + offset_by * (used - fixed)) % max(1, number_of - fixed)
        return jnp.zeros((number_of,), jnp.int32).at[sequence[jnp.where(places < fixed, places, moved)]].set(jnp.asarray(sizes, jnp.int32))

    sizes = jnp.where(number % 4 == 0, named(crowded, number // 4), named(common, number - number // 4 - 1))
    mixed = jax.random.permutation(jax.random.fold_in(own, 3), number_of)
    giver, taker = mixed[0:number_of // 2 * 2:2], mixed[1:number_of // 2 * 2:2]
    margin = jnp.minimum(sizes[giver] - 1, reach - sizes[taker]) // 2
    margin = jnp.where((giver == sequence[0]) | (taker == sequence[0]) | (sizes[taker] == 0), 0, jnp.maximum(margin, 0))
    moved = jax.random.randint(jax.random.fold_in(own, 4), (number_of // 2,), 0, 1 << 20) % (margin + 1)
    sizes = sizes.at[giver].add(-moved).at[taker].add(moved)
    items = jnp.searchsorted(jnp.cumsum(sizes), jnp.arange(rows * top), side="right").astype(jnp.int32)
    table = items.reshape(top, rows).T
    table = table[jax.random.permutation(jax.random.fold_in(own, 1), rows)]
    offset_by = jax.random.randint(jax.random.fold_in(own, 2), (rows, 1), 0, top)
    return jnp.take_along_axis(table, (jnp.arange(top)[None, :] + offset_by) % top, axis=1)


def load_shares(count, total, reach, lean, full):
    portions = [(1 << 20) // math.isqrt(grade ** lean) + 1 for grade in range(1, count + 1)]
    largest = reach if full else min(reach, max(-(-total // count), total * portions[0] // sum(portions)))
    least = 1 if total - largest >= count - 1 else 0
    counts, spare = [largest] + [least] * (count - 1), total - largest - least * (count - 1)
    while spare > 0:
        movable = [i for i in range(1, count) if counts[i] < largest] or [i for i in range(1, count) if counts[i] < reach]
        whole, remaining = sum([portions[i] for i in movable]), spare
        for i in movable:
            extra = min(reach - counts[i], max(1, remaining * portions[i] // whole), spare)
            counts[i] = counts[i] + extra
            spare = spare - extra
    return np.array(counts)


def scatter_about(stream_key, shape, width, most, cuts=(), kind=jnp.bfloat16):
    factor_of = levels(stream_key, shape, cuts, -0.22, 0.18) if cuts else 1.0
    values = jax.random.normal(stream_key, shape, jnp.float32) * width * factor_of
    return jnp.minimum(jnp.maximum(values, -most), most).astype(kind)


def setup_inputs(seed: int = 0) -> dict:
    seeds = jax.random.split(jax.random.key(seed), 10)
    forward_acts = scatter_about(seeds[0], (SECTIONS, TOKENS, D), 1.0, 6.0, ((0, 8), (1, 32)))
    forward_routes_keys = jax.random.split(jax.random.fold_in(seeds[1], 1), SECTIONS * TOKENS // TOK_DEV)
    forward_routes_turns = jax.random.permutation(jax.random.fold_in(seeds[1], 3), SECTIONS * TOKENS // TOK_DEV)
    forward_routes = jax.vmap(lambda own, number: shared_out(jax.random.fold_in(seeds[1], 2), own, number, TOK_DEV, EXPERTS, TOPK, CAP, 2))(forward_routes_keys, forward_routes_turns).reshape((SECTIONS, TOKENS, TOPK))
    forward_gates = draw_forward_gates(jax.random.fold_in(seeds[9], 71), 0)
    weight_in = scatter_about(seeds[3], (SECTIONS, EXPERTS, D, 2 * FF), D ** -0.5, 0.125, ((0, 8), (1, 32)))
    weight_down = scatter_about(seeds[4], (SECTIONS, EXPERTS, FF, D), FF ** -0.5, 0.21875, ((0, 8), (1, 32)))
    saved_acts = scatter_about(seeds[5], (SECTIONS, TOKENS, D), 1.0, 6.0, ((0, 8), (1, 32)))
    backward_routes_keys = jax.random.split(jax.random.fold_in(seeds[6], 1), SECTIONS * TOKENS // TOK_DEV)
    backward_routes_turns = jax.random.permutation(jax.random.fold_in(seeds[6], 3), SECTIONS * TOKENS // TOK_DEV)
    backward_routes = jax.vmap(lambda own, number: shared_out(jax.random.fold_in(seeds[6], 2), own, number, TOK_DEV, EXPERTS, TOPK, CAP, 2))(backward_routes_keys, backward_routes_turns).reshape((SECTIONS, TOKENS, TOPK))
    backward_gates = draw_backward_gates(jax.random.fold_in(seeds[9], 71), 0)
    sent_grads = scatter_about(seeds[8], (SECTIONS, TOKENS, D), 1.0, 6.0, ((0, 8), (1, 32)))
    return dict(forward_acts=forward_acts, forward_routes=forward_routes, forward_gates=forward_gates, weight_in=weight_in, weight_down=weight_down, saved_acts=saved_acts, backward_routes=backward_routes, backward_gates=backward_gates, sent_grads=sent_grads)


def slot_index(routes):
    blocks = routes.reshape(EXPERTS, TOK_DEV * TOPK).astype(jnp.int32)
    labels = jnp.arange(EXPERTS, dtype=jnp.int32)
    onehot = (blocks[:, :, None] == labels[None, None, :]).astype(jnp.int32)
    earlier = jnp.cumsum(onehot, axis=1) - onehot
    places = jnp.sum(earlier * onehot, axis=2)
    owners = jnp.arange(EXPERTS, dtype=jnp.int32)[:, None]
    return (blocks * (EXPERTS * CAP) + owners * CAP + places).reshape(-1).astype(jnp.int32)


def expert_forward(rows, w_in, w_down):
    both = jnp.dot(rows, w_in, preferred_element_type=jnp.float32)
    gate_part = both[:, :FF]
    up_part = both[:, FF:]
    hidden = (gate_part * jax.nn.sigmoid(gate_part) * up_part).astype(rows.dtype)
    return jnp.dot(hidden, w_down, preferred_element_type=jnp.float32).astype(rows.dtype)


def expert_backward(rows, scaled_rows, w_in, w_down):
    both = jnp.dot(rows, w_in, preferred_element_type=jnp.float32)
    gate_part = both[:, :FF]
    up_part = both[:, FF:]
    sigma = jax.nn.sigmoid(gate_part)
    hidden_grad = jnp.dot(scaled_rows, w_down.T, preferred_element_type=jnp.float32)
    gate_grad = hidden_grad * up_part * sigma * (1.0 + gate_part * (1.0 - sigma))
    up_grad = hidden_grad * gate_part * sigma
    joined = jnp.concatenate([gate_grad, up_grad], axis=1).astype(rows.dtype)
    return jnp.dot(joined, w_in.T, preferred_element_type=jnp.float32).astype(rows.dtype)


def packed(rows, index):
    empty = jnp.zeros((EXPERTS * EXPERTS * CAP, D), rows.dtype)
    return empty.at[index].set(rows).reshape(EXPERTS, EXPERTS * CAP, D)


def section_forward(group):
    acts, routes, gates, w_in, w_down = group
    index = slot_index(routes)
    owners = jnp.arange(TOKENS * TOPK, dtype=jnp.int32) // TOPK
    buffer = packed(acts[owners], index)
    results = lax.map(lambda item: expert_forward(item[0], item[1], item[2]), (buffer, w_in, w_down))
    picked = results.reshape(-1, D)[index].reshape(TOKENS, TOPK, D)
    mixed = acts.astype(jnp.float32) + jnp.einsum("tk,tkd->td", gates.astype(jnp.float32), picked.astype(jnp.float32))
    return mixed.astype(acts.dtype)


def section_backward(group):
    acts, routes, gates, grads, w_in, w_down = group
    index = slot_index(routes)
    owners = jnp.arange(TOKENS * TOPK, dtype=jnp.int32) // TOPK
    scaled = (gates.astype(jnp.float32)[:, :, None] * grads.astype(jnp.float32)[:, None, :]).astype(grads.dtype)
    buffer_acts = packed(acts[owners], index)
    buffer_grads = packed(scaled.reshape(-1, D), index)
    results = lax.map(lambda item: expert_backward(item[0], item[1], item[2], item[3]), (buffer_acts, buffer_grads, w_in, w_down))
    picked = results.reshape(-1, D)[index].reshape(TOKENS, TOPK, D)
    total = grads.astype(jnp.float32) + jnp.sum(picked.astype(jnp.float32), axis=1)
    return total.astype(grads.dtype)


def reference(forward_acts, forward_routes, forward_gates, weight_in, weight_down, saved_acts, backward_routes, backward_gates, sent_grads):
    arriving = jnp.roll(forward_acts, 1, axis=0)
    layer_out = lax.map(section_forward, (arriving, forward_routes, forward_gates, weight_in, weight_down))
    incoming = jnp.roll(sent_grads, -1, axis=0)
    input_grads = lax.map(section_backward, (saved_acts, backward_routes, backward_gates, incoming, weight_in, weight_down))
    return layer_out, input_grads
```

```python
import functools

import jax
import jax.numpy as jnp
from jax import lax
from jax.experimental import pallas as pl
from jax.experimental.pallas import tpu as pltpu
from jax.sharding import PartitionSpec as P

MESH = pl.DeviceIdType.MESH
F32 = jnp.float32
BF16 = jnp.bfloat16
D = 2048
FF = 768
TOK = 128
CAP = 16
PLANES = 4
PEERS = 8
EXPERTS = PLANES * PEERS

SAVED, GRAD, FWD = 0, 1, 2
BWD_OUT, FWD_OUT = 0, 1

DS, DG, DF, CB, CF, RB, RF, SF, FIN, META = range(10)
END_STEPS = (
    (DS, 0), (DG, 0), (META, 0), (DF, 0), (SF, 1), (CB, 0), (CF, 0), (DS, 1), (DG, 1), (CB, 1), (DS, 2), (RB, 1),
    (DG, 2), (CB, 2), (DS, 3), (RB, 2), (DG, 3), (CB, 3), (DF, 3), (RB, 3), (CF, 3), (DF, 2), (RF, 3), (CF, 2),
    (DF, 1), (RF, 2), (CF, 1), (FIN, 0), (RF, 1), (FIN, 1),
)
MID_STEPS = (
    (DS, 1), (DG, 1), (META, 0), (DS, 2), (DS, 0), (DF, 1), (DG, 2), (DG, 0), (CB, 1), (DS, 3), (DF, 0), (SF, 1),
    (CF, 1), (DG, 3), (CB, 2), (CB, 0), (DF, 3), (CB, 3), (DF, 2), (SF, 0), (CF, 0), (CF, 3), (RB, 2), (CF, 2),
    (RB, 3), (RB, 0), (RF, 3), (RF, 0), (RF, 2), (FIN, 0), (FIN, 1),
)


def lookup(step, steps):
    per = 5
    words = []
    for first in range(0, len(steps), per):
        part = steps[first : first + per]
        words.append(sum((op * 4 + block) * 64**i for i, (op, block) in enumerate(part)))
    word = jnp.int32(words[0])
    for i, w in enumerate(words[1:], 1):
        word = jnp.where(step // per == i, jnp.int32(w), word)
    place = lax.rem(step, per)
    scale = jnp.int32(1)
    for i in range(1, per):
        scale = jnp.where(place == i, jnp.int32(64**i), scale)
    return lax.rem(word // scale, 64)


def nt(a, b):
    return lax.dot_general(a, b, (((1,), (1,)), ((), ())), preferred_element_type=F32)


def nn(a, b):
    return jnp.dot(a, b, preferred_element_type=F32)


def kernel(
    meta_in, acts_in, saved_in, grads_in, w_in_hbm, w_down_hbm,
    out_f, out_b,
    gath, pk, rx, ou, rt, cin, ps, w_in, w_down, hid, joined, meta, meta_t,
    gath_sem, zs_sem, pks_sem, rx_sem, os_sem, rt_sem, cin_sem, ps_sem, meta_sem, ms_sem, w_sem, rl_sem,
):
    sec = lax.axis_index("section")
    me = lax.axis_index("expert")
    sections = lax.axis_size("section")
    z = me // PEERS
    lane = lax.rem(me, PEERS)
    ahead = lax.rem(sec + 1, sections)
    behind = lax.rem(sec + sections - 1, sections)
    flip = z >= 2
    is_mid = jnp.logical_and(z > 0, z < 3)

    def at_plane(plane):
        return (sec, plane * PEERS + lane)

    def at_peer(peer):
        return (sec, z * PEERS + peer)

    def rows(peer):
        return pl.ds(pl.multiple_of(peer * CAP, CAP), CAP)

    def remote(src, dst, send, recv, device):
        return pltpu.make_async_remote_copy(
            src_ref=src, dst_ref=dst, send_sem=send, recv_sem=recv, device_id=device, device_id_type=MESH
        )

    def wait_for(ref, sem):
        pltpu.make_async_copy(ref, ref, sem).wait()

    pltpu.make_async_copy(saved_in.at[0], gath.at[SAVED, z], gath_sem.at[SAVED, z]).start()
    load_in = pltpu.make_async_copy(w_in_hbm.at[0, 0], w_in, w_sem.at[0])
    load_down = pltpu.make_async_copy(w_down_hbm.at[0, 0], w_down, w_sem.at[1])
    load_in.start()
    load_down.start()

    barrier = pltpu.get_barrier_semaphore()
    for other in (ahead, behind):
        pl.semaphore_signal(barrier, inc=1, device_id=(other, me), device_id_type=MESH)
    for k in range(1, PLANES):
        pl.semaphore_signal(barrier, inc=1, device_id=at_plane(lax.rem(z + k, PLANES)), device_id_type=MESH)
    for k in range(1, PEERS):
        pl.semaphore_signal(barrier, inc=1, device_id=at_peer(lax.rem(lane + k, PEERS)), device_id_type=MESH)

    names = lax.broadcasted_iota(jnp.int32, (EXPERTS, TOK), 0).astype(F32)
    before = (
        lax.broadcasted_iota(jnp.int32, (TOK, TOK), 0) < lax.broadcasted_iota(jnp.int32, (TOK, TOK), 1)
    ).astype(F32).astype(BF16)
    table = meta_in[...]
    slots = []
    for first in (0, 2):
        hot = [(names == table[first + k : first + k + 1, :]).astype(F32) for k in range(2)]
        earlier = nn((hot[0] + hot[1]).astype(BF16), before)
        for k in range(2):
            place = jnp.sum(hot[k] * earlier, axis=0, keepdims=True)
            slots.append(table[first + k : first + k + 1, :] * float(CAP) + place)
    meta[z] = jnp.concatenate([*slots, table[4:8, :]], axis=0)

    pl.semaphore_wait(barrier, 2 + PLANES - 1 + PEERS - 1)

    relay_g = remote(grads_in.at[0], gath.at[GRAD, z], rl_sem.at[0], gath_sem.at[GRAD, z], (behind, me))
    relay_f = remote(acts_in.at[0], gath.at[FWD, z], rl_sem.at[1], gath_sem.at[FWD, z], (ahead, me))
    relay_g.start()
    relay_f.start()
    for k in range(1, PLANES):
        remote(meta.at[z], meta.at[z], ms_sem.at[k - 1], meta_sem.at[z], at_plane(lax.rem(z + k, PLANES))).start()

    def pass_on(t, b, right):
        return remote(
            gath.at[t, b],
            gath.at[t, b],
            zs_sem.at[t, b, 0 if right else 1],
            gath_sem.at[t, b],
            at_plane(z + 1 if right else z - 1),
        )

    def goes(b, right):
        return jnp.logical_and(b <= z, z < 3) if right else jnp.logical_and(b >= z, z > 0)

    def dispatch(t, b):
        wait_for(gath.at[t, b], gath_sem.at[t, b])
        for right in (True, False):
            cond = goes(b, right)
            if t == FWD:
                cond = jnp.logical_and(cond, b != z)

            @pl.when(cond)
            def _():
                pass_on(t, b, right).start()

        info = meta[b]
        first = 0 if t == FWD else 2
        wanted = (lax.broadcasted_iota(jnp.int32, (PEERS * CAP, TOK), 0) + z * (PEERS * CAP)).astype(F32)
        picks = [(wanted == info[first + k : first + k + 1, :]).astype(F32) for k in range(2)]
        pick = (picks[0] + picks[1]).astype(BF16)
        if t == GRAD:
            gate = jnp.sum(picks[0] * info[6:7, :] + picks[1] * info[7:8, :], axis=1, keepdims=True)
        for c in range(0, D, 512):
            part = nn(pick, gath[t, b, :, c : c + 512])
            if t == GRAD:
                part = part * gate
            pk[t, b, :, c : c + 512] = part.astype(BF16)
        for k in range(1, PEERS):
            peer = lax.rem(lane + k, PEERS)
            remote(
                pk.at[t, b, rows(peer)], rx.at[t, b, rows(lane)], pks_sem.at[t, b], rx_sem.at[t, b], at_peer(peer)
            ).start()
        pltpu.make_async_copy(pk.at[t, b, rows(lane)], rx.at[t, b, rows(lane)], rx_sem.at[t, b]).start()

    def give_back(x, b):
        for k in range(1, PEERS):
            peer = lax.rem(lane + k, PEERS)
            remote(
                ou.at[x, b, rows(peer)], rt.at[x, b, rows(lane)], os_sem.at[x, b], rt_sem.at[x, b], at_peer(peer)
            ).start()
        pltpu.make_async_copy(ou.at[x, b, rows(lane)], rt.at[x, b, rows(lane)], rt_sem.at[x, b]).start()

    def compute_forward(b):
        wait_for(rx.at[FWD, b], rx_sem.at[FWD, b])

        @pl.loop(0, FF // 256)
        def _(i):
            c = pl.multiple_of(i * 256, 256)
            x = rx[FWD, b]
            g = nn(x, w_in[:, pl.ds(c, 256)])
            u = nn(x, w_in[:, pl.ds(FF + c, 256)])
            hid[:, pl.ds(c, 256)] = (g * jax.nn.sigmoid(g) * u).astype(BF16)

        @pl.loop(0, D // 512)
        def _(i):
            c = pl.multiple_of(i * 512, 512)
            ou[FWD_OUT, b, :, pl.ds(c, 512)] = nn(hid[...], w_down[:, pl.ds(c, 512)]).astype(BF16)

        give_back(FWD_OUT, b)

    def compute_backward(b):
        wait_for(rx.at[SAVED, b], rx_sem.at[SAVED, b])
        wait_for(rx.at[GRAD, b], rx_sem.at[GRAD, b])

        @pl.loop(0, FF // 256)
        def _(i):
            c = pl.multiple_of(i * 256, 256)
            x = rx[SAVED, b]
            g = nn(x, w_in[:, pl.ds(c, 256)])
            u = nn(x, w_in[:, pl.ds(FF + c, 256)])
            h = nt(rx[GRAD, b], w_down[pl.ds(c, 256), :])
            s = jax.nn.sigmoid(g)
            joined[:, pl.ds(c, 256)] = (h * u * s * (1.0 + g * (1.0 - s))).astype(BF16)
            joined[:, pl.ds(FF + c, 256)] = (h * g * s).astype(BF16)

        @pl.loop(0, D // 256)
        def _(i):
            c = pl.multiple_of(i * 256, 256)
            ou[BWD_OUT, b, :, pl.ds(c, 256)] = nt(joined[...], w_in[pl.ds(c, 256), :]).astype(BF16)

        give_back(BWD_OUT, b)

    def weights_of(x, b):
        info = meta_t[b]
        wanted = (lax.broadcasted_iota(jnp.int32, (TOK, PEERS * CAP), 1) + z * (PEERS * CAP)).astype(F32)
        first = 0 if x == FWD_OUT else 2
        picks = [(wanted == info[:, first + k : first + k + 1]).astype(F32) for k in range(2)]
        if x == BWD_OUT:
            return [(picks[0] + picks[1]).astype(BF16)]
        full = picks[0] * info[:, 4:5] + picks[1] * info[:, 5:6]
        high = full.astype(BF16)
        return [high, (full - high.astype(F32)).astype(BF16)]

    def summed(x, b, weights, c):
        value = rt[x, b, :, c : c + 512]
        total = nn(weights[0], value)
        for w in weights[1:]:
            total = total + nn(w, value)
        return total

    def chain_out(x, b):
        right = b > z
        plane = jnp.where(right, z + 1, z - 1)
        slot = jnp.where(jnp.logical_and(jnp.logical_not(right), plane == b), 4, b)
        return remote(ps.at[x, b], cin.at[x, slot], ps_sem.at[x, b], cin_sem.at[x, slot], at_plane(plane))

    def reduce_step(x, b):
        wait_for(rt.at[x, b], rt_sem.at[x, b])
        weights = weights_of(x, b)
        has = is_mid

        @pl.when(has)
        def _():
            wait_for(cin.at[x, b], cin_sem.at[x, b])
            for c in range(0, D, 512):
                ps[x, b, :, c : c + 512] = (
                    summed(x, b, weights, c) + cin[x, b, :, c : c + 512].astype(F32)
                ).astype(BF16)

        @pl.when(jnp.logical_not(has))
        def _():
            for c in range(0, D, 512):
                ps[x, b, :, c : c + 512] = summed(x, b, weights, c).astype(BF16)

        chain_out(x, b).start()

    def finish(x):
        out = out_b if x == BWD_OUT else out_f
        t = GRAD if x == BWD_OUT else FWD
        wait_for(rt.at[x, z], rt_sem.at[x, z])
        weights = weights_of(x, z)

        @pl.when(z > 0)
        def _():
            wait_for(cin.at[x, z], cin_sem.at[x, z])

        @pl.when(z < 3)
        def _():
            wait_for(cin.at[x, 4], cin_sem.at[x, 4])

        for c in range(0, D, 512):
            total = gath[t, z, :, c : c + 512].astype(F32) + summed(x, z, weights, c)
            left = jnp.where(z > 0, cin[x, z, :, c : c + 512].astype(F32), 0.0)
            right = jnp.where(z < 3, cin[x, 4, :, c : c + 512].astype(F32), 0.0)
            out[0, :, c : c + 512] = (total + left + right).astype(BF16)

    def every_meta():
        for k in range(1, PLANES):
            b = lax.rem(z + k, PLANES)
            wait_for(meta.at[b], meta_sem.at[b])
        for b in range(PLANES):
            meta_t[b] = jnp.concatenate([meta[b]] * (TOK // 8), axis=0).T
        load_in.wait()
        load_down.wait()

    def own_forward(d):
        rightward = jnp.logical_xor(d == 1, flip)

        @pl.when(jnp.logical_and(rightward, z < 3))
        def _():
            pass_on(FWD, z, True).start()

        @pl.when(jnp.logical_and(jnp.logical_not(rightward), z > 0))
        def _():
            pass_on(FWD, z, False).start()

    n_steps = max(len(END_STEPS), len(MID_STEPS))
    n_mine = jnp.where(is_mid, len(MID_STEPS), len(END_STEPS))

    @pl.loop(0, n_steps)
    def _(i):
        code = jnp.where(is_mid, lookup(i, MID_STEPS), lookup(i, END_STEPS))
        code = jnp.where(i < n_mine, code, 63)
        op = code // 4
        raw = lax.rem(code, 4)
        b = jnp.where(flip, 3 - raw, raw)

        for number, run in (
            (DS, lambda: dispatch(SAVED, b)),
            (DG, lambda: dispatch(GRAD, b)),
            (DF, lambda: dispatch(FWD, b)),
            (CB, lambda: compute_backward(b)),
            (CF, lambda: compute_forward(b)),
            (RB, lambda: reduce_step(BWD_OUT, b)),
            (RF, lambda: reduce_step(FWD_OUT, b)),
            (SF, lambda: own_forward(raw)),
            (META, every_meta),
        ):
            pl.when(op == number)(run)
        pl.when(jnp.logical_and(op == FIN, raw == 0))(lambda: finish(BWD_OUT))
        pl.when(jnp.logical_and(op == FIN, raw == 1))(lambda: finish(FWD_OUT))

    relay_g.wait_send()
    relay_f.wait_send()
    for k in range(1, PLANES):
        remote(meta.at[z], meta.at[z], ms_sem.at[k - 1], meta_sem.at[z], at_plane(lax.rem(z + k, PLANES))).wait_send()
    sent = pl.ds(0, (PEERS - 1) * CAP)
    for b in range(PLANES):
        for t in range(3):
            for right in (True, False):

                @pl.when(goes(b, right))
                def _():
                    pass_on(t, b, right).wait_send()

            wait_for(pk.at[t, b, sent], pks_sem.at[t, b])
        for x in range(2):
            wait_for(ou.at[x, b, sent], os_sem.at[x, b])

            @pl.when(b != z)
            def _():
                wait_for(ps.at[x, b], ps_sem.at[x, b])


def per_device(acts, f_routes, f_gates, w_in, w_down, saved, b_routes, b_gates, grads):
    table = jnp.concatenate(
        [f_routes[0].T.astype(F32), b_routes[0].T.astype(F32), f_gates[0].T, b_gates[0].T], axis=0
    )
    dma = pltpu.SemaphoreType.DMA
    block = (TOK, D)
    out = jax.ShapeDtypeStruct((1, TOK, D), BF16)
    vmem = pl.BlockSpec(memory_space=pltpu.VMEM)
    hbm = pl.BlockSpec(memory_space=pl.ANY)
    return tuple(
        pl.pallas_call(
            kernel,
            name="moe_relay",
            out_shape=(out, out),
            in_specs=[vmem, hbm, hbm, hbm, hbm, hbm],
            out_specs=(vmem, vmem),
            scratch_shapes=[
                pltpu.VMEM((3, PLANES, *block), BF16),
                pltpu.VMEM((3, PLANES, *block), BF16),
                pltpu.VMEM((3, PLANES, *block), BF16),
                pltpu.VMEM((2, PLANES, *block), BF16),
                pltpu.VMEM((2, PLANES, *block), BF16),
                pltpu.VMEM((2, PLANES + 1, *block), BF16),
                pltpu.VMEM((2, PLANES, *block), BF16),
                pltpu.VMEM((D, 2 * FF), BF16),
                pltpu.VMEM((FF, D), BF16),
                pltpu.VMEM((TOK, FF), BF16),
                pltpu.VMEM((TOK, 2 * FF), BF16),
                pltpu.VMEM((PLANES, 8, TOK), F32),
                pltpu.VMEM((PLANES, TOK, TOK), F32),
                dma((3, PLANES)),
                dma((3, PLANES, 2)),
                dma((3, PLANES)),
                dma((3, PLANES)),
                dma((2, PLANES)),
                dma((2, PLANES)),
                dma((2, PLANES + 1)),
                dma((2, PLANES)),
                dma((PLANES,)),
                dma((PLANES - 1,)),
                dma((2,)),
                dma((2,)),
            ],
            compiler_params=pltpu.CompilerParams(
                collective_id=0, has_side_effects=True, vmem_limit_bytes=60 * 2**20
            ),
        )(table, acts, saved, grads, w_in, w_down)
    )


def solution(mesh):
    rows = P("section", "expert", None)
    weights = P("section", "expert", None, None)
    return jax.shard_map(
        per_device,
        mesh=mesh,
        in_specs=(rows, rows, rows, weights, weights, rows, rows, rows, rows),
        out_specs=(rows, rows),
        check_vma=False,
    )
```

```python
import functools

import jax
import jax.numpy as jnp
from jax import lax
from jax.experimental import pallas as pl
from jax.experimental.pallas import tpu as pltpu
from jax.sharding import PartitionSpec as P

MESH = pl.DeviceIdType.MESH
F32 = jnp.float32
BF16 = jnp.bfloat16
D = 2048
FF = 768
TOK = 128
CAP = 16
PLANES = 4
PEERS = 8
EXPERTS = PLANES * PEERS

SAVED, GRAD, FWD = 0, 1, 2
BWD_OUT, FWD_OUT = 0, 1

TAKE, PACK, OWN, MAKE_B, MAKE_F, SUM_B, SUM_F, FINISH, TABLES, ACROSS, LAST = 0, 12, 24, 30, 34, 38, 42, 46, 48, 49, 51
END_INNER = (
    0, 48, 25, 4, 8, 16, 20, 27, 1, 12, 5, 17, 2, 29, 13, 14, 6, 18, 31, 32,
    3, 7, 19, 15, 40, 11, 39, 23, 33, 28, 10, 37, 22, 41, 30, 45, 36, 9, 26, 24,
    21, 44, 35, 43, 34, 47, 46,
)
MID_INNER = (
    1, 25, 24, 48, 5, 26, 27, 13, 0, 17, 2, 4, 9, 6, 16, 3, 12, 31, 7, 8,
    14, 20, 18, 30, 19, 15, 29, 11, 10, 23, 32, 28, 33, 40, 22, 34, 37, 41, 36, 45,
    21, 38, 42, 44, 46, 35, 47,
)
END_FIRST = (
    1, 0, 25, 4, 49, 48, 12, 16, 11, 23, 24, 37, 27, 5, 13, 50, 17, 2, 10, 14,
    31, 3, 15, 6, 18, 45, 39, 7, 19, 32, 33, 40, 22, 8, 20, 41, 36, 9, 26, 21,
    44, 35, 30, 43, 34, 47, 46,
)
MID_FIRST = (
    1, 24, 25, 13, 5, 26, 27, 49, 17, 48, 31, 2, 0, 12, 3, 14, 11, 4, 6, 18,
    16, 23, 7, 10, 15, 32, 19, 9, 37, 30, 8, 20, 33, 22, 45, 40, 34, 41, 21, 42,
    36, 46, 38, 44, 35, 47,
)
END_LAST = (
    48, 0, 25, 1, 8, 20, 12, 29, 49, 50, 7, 13, 19, 6, 2, 14, 18, 10, 22, 36,
    3, 15, 28, 32, 44, 11, 34, 23, 33, 40, 5, 17, 41, 37, 31, 45, 9, 21, 24, 4,
    16, 39, 35, 30, 43, 46, 47,
)
MID_LAST = (
    1, 25, 24, 49, 9, 29, 0, 48, 12, 2, 14, 8, 10, 20, 22, 13, 3, 15, 34, 6,
    11, 36, 23, 18, 5, 7, 19, 28, 4, 16, 17, 44, 32, 33, 31, 37, 41, 30, 45, 21,
    38, 35, 42, 40, 47, 46,
)


def lookup(step, choices):
    per = 5
    longest = max(len(steps) for _, steps in choices)
    words = []
    for first in range(0, longest, per):
        word = None
        for cond, steps in reversed(choices):
            part = [*steps[first : first + per]]
            part += [LAST] * (per - len(part))
            here = jnp.int32(sum(number * 64**i for i, number in enumerate(part)))
            word = here if word is None else jnp.where(cond, here, word)
        words.append(word)
    word = words[0]
    for i, w in enumerate(words[1:], 1):
        word = jnp.where(step // per == i, w, word)
    place = lax.rem(step, per)
    scale = jnp.int32(1)
    for i in range(1, per):
        scale = jnp.where(place == i, jnp.int32(64**i), scale)
    return lax.rem(word // scale, 64)


def nt(a, b):
    return lax.dot_general(a, b, (((1,), (1,)), ((), ())), preferred_element_type=F32)


def nn(a, b):
    return jnp.dot(a, b, preferred_element_type=F32)


def kernel(
    meta_in, acts_in, saved_in, grads_in, w_in_hbm, w_down_hbm,
    out_f, out_b,
    gath, held, pk, rx, ou, rt, cin, ps, w_in, w_down, hid, joined, meta, meta_t,
    gath_sem, held_sem, ac_sem, zs_sem, pks_sem, rx_sem, os_sem, rt_sem, cin_sem, ps_sem, meta_sem, ms_sem, w_sem, rl_sem,
):
    sec = lax.axis_index("section")
    me = lax.axis_index("expert")
    z = me // PEERS
    lane = lax.rem(me, PEERS)
    half = sec // 4
    x = lax.rem(sec, 4)
    ahead = half * 4 + lax.rem(x + 1, 4)
    behind = half * 4 + lax.rem(x + 3, 4)
    first, last = x == 0, x == 3
    crossing = jnp.logical_or(first, last)
    across = (lax.rem(sec + 4, 8), (3 - z) * PEERS + lane)
    flip = z >= 2
    is_mid = jnp.logical_and(z > 0, z < 3)
    is_end = jnp.logical_not(is_mid)

    def crosses(t):
        return jnp.logical_or(jnp.logical_and(t == FWD, first), jnp.logical_and(t == GRAD, last))

    def at_plane(plane):
        return (sec, plane * PEERS + lane)

    def at_peer(peer):
        return (sec, z * PEERS + peer)

    def rows(peer):
        return pl.ds(pl.multiple_of(peer * CAP, CAP), CAP)

    def remote(src, dst, send, recv, device):
        return pltpu.make_async_remote_copy(
            src_ref=src, dst_ref=dst, send_sem=send, recv_sem=recv, device_id=device, device_id_type=MESH
        )

    def wait_for(ref, sem):
        pltpu.make_async_copy(ref, ref, sem).wait()

    pltpu.make_async_copy(saved_in.at[0], gath.at[SAVED, z], gath_sem.at[SAVED, z]).start()
    load_in = pltpu.make_async_copy(w_in_hbm.at[0, 0], w_in, w_sem.at[0])
    load_down = pltpu.make_async_copy(w_down_hbm.at[0, 0], w_down, w_sem.at[1])
    load_in.start()
    load_down.start()

    barrier = pltpu.get_barrier_semaphore()
    for other in (ahead, behind):
        pl.semaphore_signal(barrier, inc=1, device_id=(other, me), device_id_type=MESH)
    for k in range(1, PLANES):
        pl.semaphore_signal(barrier, inc=1, device_id=at_plane(lax.rem(z + k, PLANES)), device_id_type=MESH)
    for k in range(1, PEERS):
        pl.semaphore_signal(barrier, inc=1, device_id=at_peer(lax.rem(lane + k, PEERS)), device_id_type=MESH)

    @pl.when(jnp.logical_and(crossing, is_end))
    def _():
        pl.semaphore_signal(barrier, inc=1, device_id=across, device_id_type=MESH)

    names = lax.broadcasted_iota(jnp.int32, (EXPERTS, TOK), 0).astype(F32)
    before = (
        lax.broadcasted_iota(jnp.int32, (TOK, TOK), 0) < lax.broadcasted_iota(jnp.int32, (TOK, TOK), 1)
    ).astype(F32).astype(BF16)
    table = meta_in[...]
    slots = []
    for row in (0, 2):
        hot = [(names == table[row + k : row + k + 1, :]).astype(F32) for k in range(2)]
        earlier = nn((hot[0] + hot[1]).astype(BF16), before)
        for k in range(2):
            place = jnp.sum(hot[k] * earlier, axis=0, keepdims=True)
            slots.append(table[row + k : row + k + 1, :] * float(CAP) + place)
    meta[z] = jnp.concatenate([*slots, table[4:8, :]], axis=0)

    partners = 2 + PLANES - 1 + PEERS - 1
    pl.semaphore_wait(barrier, jnp.where(jnp.logical_and(crossing, is_end), partners + 1, partners))

    def relay(t, to, stops, stop):
        source = grads_in if t == GRAD else acts_in
        number = 0 if t == GRAD else 1
        target, sem = (held, held_sem) if stop else (gath.at[t], gath_sem.at[t])
        return remote(source.at[0], target.at[z], rl_sem.at[number], sem.at[z], (to, me))

    for t, to, stops in ((GRAD, behind, first), (FWD, ahead, last)):
        pl.when(stops)(lambda: relay(t, to, stops, True).start())
        pl.when(jnp.logical_not(stops))(lambda: relay(t, to, stops, False).start())
    for k in range(1, PLANES):
        remote(meta.at[z], meta.at[z], ms_sem.at[k - 1], meta_sem.at[z], at_plane(lax.rem(z + k, PLANES))).start()

    def pass_on(t, b, right):
        return remote(
            gath.at[t, b],
            gath.at[t, b],
            zs_sem.at[t, b, 0 if right else 1],
            gath_sem.at[t, b],
            at_plane(z + 1 if right else z - 1),
        )

    def goes(t, b, right, own):
        far = b >= 2 if right else b < 2
        if own:
            near = b <= z if right else b >= z
        else:
            near = b < z if right else b > z
        there = z < 3 if right else z > 0
        hot = crosses(t)
        wanted = jnp.logical_or(jnp.logical_and(hot, far), jnp.logical_and(jnp.logical_not(hot), near))
        return jnp.logical_and(wanted, there)

    def take(t, b):
        wait_for(gath.at[t, b], gath_sem.at[t, b])
        for right in (True, False):
            pl.when(goes(t, b, right, False))(lambda: pass_on(t, b, right).start())

    def own(t, d):
        rightward = jnp.logical_xor(d == 1, flip)
        pl.when(jnp.logical_and(rightward, z < 3))(lambda: pass_on(t, z, True).start())
        pl.when(jnp.logical_and(jnp.logical_not(rightward), z > 0))(lambda: pass_on(t, z, False).start())

    def held_on(b, k):
        return remote(held.at[b], held.at[b], ac_sem.at[k], held_sem.at[b], at_plane(jnp.where(flip, z + 1, z - 1)))

    def held_across(b, k):
        t = jnp.where(first, FWD, GRAD)
        return remote(held.at[b], gath.at[t, b], ac_sem.at[k], gath_sem.at[t, b], across)

    def send_held(k):
        b = jnp.where(k == 0, z, jnp.where(flip, 2, 1))
        wait_for(held.at[b], held_sem.at[b])
        pl.when(is_end)(lambda: held_across(b, k).start())
        pl.when(is_mid)(lambda: held_on(b, k).start())

    def pack(t, b):
        info = meta[b]
        wanted = (lax.broadcasted_iota(jnp.int32, (PEERS * CAP, TOK), 0) + z * (PEERS * CAP)).astype(F32)
        forward = t == FWD
        picks = [
            (wanted == jnp.where(forward, info[k : k + 1, :], info[2 + k : 3 + k, :])).astype(F32) for k in range(2)
        ]
        pick = (picks[0] + picks[1]).astype(BF16)
        gate = jnp.sum(picks[0] * info[6:7, :] + picks[1] * info[7:8, :], axis=1, keepdims=True)
        gate = jnp.where(t == GRAD, gate, 1.0)
        for c in range(0, D, 512):
            pk[t, b, :, c : c + 512] = (nn(pick, gath[t, b, :, c : c + 512]) * gate).astype(BF16)
        for k in range(1, PEERS):
            peer = lax.rem(lane + k, PEERS)
            remote(
                pk.at[t, b, rows(peer)], rx.at[t, b, rows(lane)], pks_sem.at[t, b], rx_sem.at[t, b], at_peer(peer)
            ).start()
        pltpu.make_async_copy(pk.at[t, b, rows(lane)], rx.at[t, b, rows(lane)], rx_sem.at[t, b]).start()

    def give_back(x, b):
        for k in range(1, PEERS):
            peer = lax.rem(lane + k, PEERS)
            remote(
                ou.at[x, b, rows(peer)], rt.at[x, b, rows(lane)], os_sem.at[x, b], rt_sem.at[x, b], at_peer(peer)
            ).start()
        pltpu.make_async_copy(ou.at[x, b, rows(lane)], rt.at[x, b, rows(lane)], rt_sem.at[x, b]).start()

    def compute_forward(b):
        wait_for(rx.at[FWD, b], rx_sem.at[FWD, b])

        @pl.loop(0, FF // 256)
        def _(i):
            c = pl.multiple_of(i * 256, 256)
            x = rx[FWD, b]
            g = nn(x, w_in[:, pl.ds(c, 256)])
            u = nn(x, w_in[:, pl.ds(FF + c, 256)])
            hid[:, pl.ds(c, 256)] = (g * jax.nn.sigmoid(g) * u).astype(BF16)

        @pl.loop(0, D // 512)
        def _(i):
            c = pl.multiple_of(i * 512, 512)
            ou[FWD_OUT, b, :, pl.ds(c, 512)] = nn(hid[...], w_down[:, pl.ds(c, 512)]).astype(BF16)

        give_back(FWD_OUT, b)

    def compute_backward(b):
        wait_for(rx.at[SAVED, b], rx_sem.at[SAVED, b])
        wait_for(rx.at[GRAD, b], rx_sem.at[GRAD, b])

        @pl.loop(0, FF // 256)
        def _(i):
            c = pl.multiple_of(i * 256, 256)
            x = rx[SAVED, b]
            g = nn(x, w_in[:, pl.ds(c, 256)])
            u = nn(x, w_in[:, pl.ds(FF + c, 256)])
            h = nt(rx[GRAD, b], w_down[pl.ds(c, 256), :])
            s = jax.nn.sigmoid(g)
            joined[:, pl.ds(c, 256)] = (h * u * s * (1.0 + g * (1.0 - s))).astype(BF16)
            joined[:, pl.ds(FF + c, 256)] = (h * g * s).astype(BF16)

        @pl.loop(0, D // 256)
        def _(i):
            c = pl.multiple_of(i * 256, 256)
            ou[BWD_OUT, b, :, pl.ds(c, 256)] = nt(joined[...], w_in[pl.ds(c, 256), :]).astype(BF16)

        give_back(BWD_OUT, b)

    def weights_of(x, b):
        info = meta_t[b]
        wanted = (lax.broadcasted_iota(jnp.int32, (TOK, PEERS * CAP), 1) + z * (PEERS * CAP)).astype(F32)
        first = 0 if x == FWD_OUT else 2
        picks = [(wanted == info[:, first + k : first + k + 1]).astype(F32) for k in range(2)]
        if x == BWD_OUT:
            return [(picks[0] + picks[1]).astype(BF16)]
        full = picks[0] * info[:, 4:5] + picks[1] * info[:, 5:6]
        high = full.astype(BF16)
        return [high, (full - high.astype(F32)).astype(BF16)]

    def summed(x, b, weights, c):
        value = rt[x, b, :, c : c + 512]
        total = nn(weights[0], value)
        for w in weights[1:]:
            total = total + nn(w, value)
        return total

    def chain_out(x, b):
        right = b > z
        plane = jnp.where(right, z + 1, z - 1)
        slot = jnp.where(jnp.logical_and(jnp.logical_not(right), plane == b), 4, b)
        return remote(ps.at[x, b], cin.at[x, slot], ps_sem.at[x, b], cin_sem.at[x, slot], at_plane(plane))

    def reduce_step(x, b):
        wait_for(rt.at[x, b], rt_sem.at[x, b])
        weights = weights_of(x, b)
        has = is_mid

        @pl.when(has)
        def _():
            wait_for(cin.at[x, b], cin_sem.at[x, b])
            for c in range(0, D, 512):
                ps[x, b, :, c : c + 512] = (
                    summed(x, b, weights, c) + cin[x, b, :, c : c + 512].astype(F32)
                ).astype(BF16)

        @pl.when(jnp.logical_not(has))
        def _():
            for c in range(0, D, 512):
                ps[x, b, :, c : c + 512] = summed(x, b, weights, c).astype(BF16)

        chain_out(x, b).start()

    def finish(x):
        out = out_b if x == BWD_OUT else out_f
        t = GRAD if x == BWD_OUT else FWD
        wait_for(rt.at[x, z], rt_sem.at[x, z])
        weights = weights_of(x, z)

        @pl.when(z > 0)
        def _():
            wait_for(cin.at[x, z], cin_sem.at[x, z])

        @pl.when(z < 3)
        def _():
            wait_for(cin.at[x, 4], cin_sem.at[x, 4])

        for c in range(0, D, 512):
            total = gath[t, z, :, c : c + 512].astype(F32) + summed(x, z, weights, c)
            left = jnp.where(z > 0, cin[x, z, :, c : c + 512].astype(F32), 0.0)
            right = jnp.where(z < 3, cin[x, 4, :, c : c + 512].astype(F32), 0.0)
            out[0, :, c : c + 512] = (total + left + right).astype(BF16)

    def every_meta():
        for k in range(1, PLANES):
            b = lax.rem(z + k, PLANES)
            wait_for(meta.at[b], meta_sem.at[b])
        for b in range(PLANES):
            meta_t[b] = jnp.concatenate([meta[b]] * (TOK // 8), axis=0).T
        load_in.wait()
        load_down.wait()

    end_tables = [(first, END_FIRST), (last, END_LAST), (None, END_INNER)]
    mid_tables = [(first, MID_FIRST), (last, MID_LAST), (None, MID_INNER)]
    choices = [(jnp.logical_and(is_mid, c) if c is not None else is_mid, steps) for c, steps in mid_tables]
    choices += end_tables

    def seen(raw):
        return jnp.where(flip, 3 - raw, raw)

    @pl.loop(0, max(len(steps) for _, steps in choices))
    def _(i):
        code = lookup(i, choices)

        def during(start, end, run):
            pl.when(jnp.logical_and(code >= start, code < end))(lambda: run(code - start))

        during(TAKE, PACK, lambda n: take(n // 4, seen(lax.rem(n, 4))))
        during(PACK, OWN, lambda n: pack(n // 4, seen(lax.rem(n, 4))))
        during(OWN, MAKE_B, lambda n: own(n // 2, lax.rem(n, 2)))
        during(MAKE_B, MAKE_F, lambda n: compute_backward(seen(n)))
        during(MAKE_F, SUM_B, lambda n: compute_forward(seen(n)))
        during(SUM_B, SUM_F, lambda n: reduce_step(BWD_OUT, seen(n)))
        during(SUM_F, FINISH, lambda n: reduce_step(FWD_OUT, seen(n)))
        during(FINISH, FINISH + 1, lambda n: finish(BWD_OUT))
        during(FINISH + 1, TABLES, lambda n: finish(FWD_OUT))
        during(TABLES, ACROSS, lambda n: every_meta())
        during(ACROSS, LAST, send_held)

    wait_for(held.at[z], rl_sem.at[0])
    wait_for(held.at[z], rl_sem.at[1])
    pl.when(crossing)(lambda: wait_for(held.at[z], ac_sem.at[0]))
    pl.when(jnp.logical_and(crossing, is_end))(lambda: wait_for(held.at[z], ac_sem.at[1]))
    for k in range(1, PLANES):
        remote(meta.at[z], meta.at[z], ms_sem.at[k - 1], meta_sem.at[z], at_plane(lax.rem(z + k, PLANES))).wait_send()
    sent = pl.ds(0, (PEERS - 1) * CAP)
    for b in range(PLANES):
        for t in range(3):
            for right in (True, False):
                pl.when(goes(t, b, right, True))(lambda: pass_on(t, b, right).wait_send())

            wait_for(pk.at[t, b, sent], pks_sem.at[t, b])
        for x in range(2):
            wait_for(ou.at[x, b, sent], os_sem.at[x, b])

            @pl.when(b != z)
            def _():
                wait_for(ps.at[x, b], ps_sem.at[x, b])


def per_device(acts, f_routes, f_gates, w_in, w_down, saved, b_routes, b_gates, grads):
    table = jnp.concatenate(
        [f_routes[0].T.astype(F32), b_routes[0].T.astype(F32), f_gates[0].T, b_gates[0].T], axis=0
    )
    dma = pltpu.SemaphoreType.DMA
    block = (TOK, D)
    out = jax.ShapeDtypeStruct((1, TOK, D), BF16)
    vmem = pl.BlockSpec(memory_space=pltpu.VMEM)
    hbm = pl.BlockSpec(memory_space=pl.ANY)
    return tuple(
        pl.pallas_call(
            kernel,
            name="moe_relay",
            out_shape=(out, out),
            in_specs=[vmem, hbm, hbm, hbm, hbm, hbm],
            out_specs=(vmem, vmem),
            scratch_shapes=[
                pltpu.VMEM((3, PLANES, *block), BF16),
                pltpu.VMEM((PLANES, *block), BF16),
                pltpu.VMEM((3, PLANES, *block), BF16),
                pltpu.VMEM((3, PLANES, *block), BF16),
                pltpu.VMEM((2, PLANES, *block), BF16),
                pltpu.VMEM((2, PLANES, *block), BF16),
                pltpu.VMEM((2, PLANES + 1, *block), BF16),
                pltpu.VMEM((2, PLANES, *block), BF16),
                pltpu.VMEM((D, 2 * FF), BF16),
                pltpu.VMEM((FF, D), BF16),
                pltpu.VMEM((TOK, FF), BF16),
                pltpu.VMEM((TOK, 2 * FF), BF16),
                pltpu.VMEM((PLANES, 8, TOK), F32),
                pltpu.VMEM((PLANES, TOK, TOK), F32),
                dma((3, PLANES)),
                dma((PLANES,)),
                dma((2,)),
                dma((3, PLANES, 2)),
                dma((3, PLANES)),
                dma((3, PLANES)),
                dma((2, PLANES)),
                dma((2, PLANES)),
                dma((2, PLANES + 1)),
                dma((2, PLANES)),
                dma((PLANES,)),
                dma((PLANES - 1,)),
                dma((2,)),
                dma((2,)),
            ],
            compiler_params=pltpu.CompilerParams(
                collective_id=0, has_side_effects=True, vmem_limit_bytes=60 * 2**20
            ),
        )(table, acts, saved, grads, w_in, w_down)
    )


def solution(mesh):
    rows = P("section", "expert", None)
    weights = P("section", "expert", None, None)
    return jax.shard_map(
        per_device,
        mesh=mesh,
        in_specs=(rows, rows, rows, weights, weights, rows, rows, rows, rows),
        out_specs=(rows, rows),
        check_vma=False,
    )
```

```python
import functools

import jax
import jax.numpy as jnp
from jax import lax
from jax.experimental import pallas as pl
from jax.experimental.pallas import tpu as pltpu
from jax.sharding import PartitionSpec as P

MESH = pl.DeviceIdType.MESH
F32 = jnp.float32
BF16 = jnp.bfloat16
D = 2048
FF = 768
TOK = 128
CAP = 16
PLANES = 4
PEERS = 8
EXPERTS = PLANES * PEERS

SAVED, GRAD, FWD = 0, 1, 2
BWD_OUT, FWD_OUT = 0, 1

TAKE, PACK, PACK_OUT, OWN, MAKE_B, MAKE_F = 0, 12, 24, 36, 39, 43
SUM_B, SUM_F, FINISH, TABLES, ACROSS, LAST = 47, 51, 55, 57, 58, 60
END_INNER = (
    0, 12, 36, 4, 8, 37, 57, 38, 20, 16, 40, 48, 41, 49, 42, 50, 46, 54, 45, 53,
    44, 43, 39, 52, 55, 56,
)
MID_INNER = (
    1, 36, 25, 5, 29, 2, 37, 9, 57, 14, 21, 26, 0, 12, 17, 6, 30, 4, 3, 18,
    15, 16, 27, 8, 7, 31, 19, 11, 20, 38, 23, 41, 35, 10, 42, 34, 22, 49, 46, 39,
    33, 50, 13, 45, 54, 47, 43, 40, 53, 51, 44, 55, 56,
)
END_FIRST = (
    0, 57, 36, 12, 58, 4, 16, 37, 11, 23, 59, 46, 10, 22, 54, 41, 49, 45, 42, 53,
    50, 40, 8, 20, 48, 44, 43, 39, 52, 56, 55,
)
MID_FIRST = (
    1, 25, 36, 5, 37, 58, 17, 57, 13, 2, 14, 26, 0, 6, 18, 30, 4, 16, 3, 11,
    15, 27, 23, 12, 7, 31, 19, 46, 10, 29, 22, 41, 8, 9, 20, 54, 21, 33, 42, 49,
    43, 39, 50, 51, 45, 40, 53, 47, 44, 55, 56,
)
END_LAST = (
    0, 36, 58, 8, 20, 57, 38, 12, 7, 19, 59, 44, 6, 18, 52, 45, 42, 53, 50, 4,
    46, 54, 41, 49, 16, 40, 39, 48, 43, 55, 56,
)
MID_LAST = (
    1, 36, 25, 13, 58, 57, 2, 9, 38, 33, 14, 21, 10, 0, 22, 44, 34, 12, 7, 19,
    3, 45, 27, 15, 8, 4, 16, 20, 11, 6, 23, 35, 42, 5, 26, 53, 18, 39, 29, 46,
    50, 41, 43, 54, 47, 56, 17, 49, 51, 40, 55,
)


def lookup(step, choices):
    per = 5
    longest = max(len(steps) for _, steps in choices)
    words = []
    for first in range(0, longest, per):
        word = None
        for cond, steps in reversed(choices):
            part = [*steps[first : first + per]]
            part += [LAST] * (per - len(part))
            here = jnp.int32(sum(number * 64**i for i, number in enumerate(part)))
            word = here if word is None else jnp.where(cond, here, word)
        words.append(word)
    word = words[0]
    for i, w in enumerate(words[1:], 1):
        word = jnp.where(step // per == i, w, word)
    place = lax.rem(step, per)
    scale = jnp.int32(1)
    for i in range(1, per):
        scale = jnp.where(place == i, jnp.int32(64**i), scale)
    return lax.rem(word // scale, 64)


def nt(a, b):
    return lax.dot_general(a, b, (((1,), (1,)), ((), ())), preferred_element_type=F32)


def nn(a, b):
    return jnp.dot(a, b, preferred_element_type=F32)


def kernel(
    meta_in, acts_in, saved_in, grads_in, w_in_hbm, w_down_hbm,
    out_f, out_b,
    gath, held, pk, pk_out, rx, ou, rt, cin, ps, w_in, w_down, hid, joined, meta, meta_t,
    gath_sem, held_sem, ac_sem, zs_sem, pks_sem, pko_sem, rx_sem, os_sem, rt_sem, cin_sem, ps_sem, meta_sem, ms_sem, w_sem, rl_sem,
):
    sec = lax.axis_index("section")
    me = lax.axis_index("expert")
    z = me // PEERS
    lane = lax.rem(me, PEERS)
    half = sec // 4
    x = lax.rem(sec, 4)
    ahead = half * 4 + lax.rem(x + 1, 4)
    behind = half * 4 + lax.rem(x + 3, 4)
    first, last = x == 0, x == 3
    crossing = jnp.logical_or(first, last)
    across = (lax.rem(sec + 4, 8), (3 - z) * PEERS + lane)
    flip = z >= 2
    is_mid = jnp.logical_and(z > 0, z < 3)
    is_end = jnp.logical_not(is_mid)

    def crosses(t):
        return jnp.logical_or(jnp.logical_and(t == FWD, first), jnp.logical_and(t == GRAD, last))

    def at_plane(plane):
        return (sec, plane * PEERS + lane)

    def at_peer(peer):
        return (sec, z * PEERS + peer)

    def rows(peer):
        return pl.ds(pl.multiple_of(peer * CAP, CAP), CAP)

    def remote(src, dst, send, recv, device):
        return pltpu.make_async_remote_copy(
            src_ref=src, dst_ref=dst, send_sem=send, recv_sem=recv, device_id=device, device_id_type=MESH
        )

    def wait_for(ref, sem):
        pltpu.make_async_copy(ref, ref, sem).wait()

    pltpu.make_async_copy(saved_in.at[0], gath.at[SAVED, z], gath_sem.at[SAVED, z]).start()
    load_in = pltpu.make_async_copy(w_in_hbm.at[0, 0], w_in, w_sem.at[0])
    load_down = pltpu.make_async_copy(w_down_hbm.at[0, 0], w_down, w_sem.at[1])
    load_in.start()
    load_down.start()

    pair = z + 1 - 2 * lax.rem(z, 2)
    barrier = pltpu.get_barrier_semaphore()
    for other in (ahead, behind):
        pl.semaphore_signal(barrier, inc=1, device_id=(other, me), device_id_type=MESH)
    for k in range(1, PLANES):
        pl.semaphore_signal(barrier, inc=1, device_id=at_plane(lax.rem(z + k, PLANES)), device_id_type=MESH)
    for k in range(1, PEERS):
        peer = lax.rem(lane + k, PEERS)
        pl.semaphore_signal(barrier, inc=1, device_id=at_peer(peer), device_id_type=MESH)
        pl.semaphore_signal(barrier, inc=1, device_id=(sec, pair * PEERS + peer), device_id_type=MESH)

    @pl.when(jnp.logical_and(crossing, is_end))
    def _():
        pl.semaphore_signal(barrier, inc=1, device_id=across, device_id_type=MESH)

    names = lax.broadcasted_iota(jnp.int32, (EXPERTS, TOK), 0).astype(F32)
    before = (
        lax.broadcasted_iota(jnp.int32, (TOK, TOK), 0) < lax.broadcasted_iota(jnp.int32, (TOK, TOK), 1)
    ).astype(F32).astype(BF16)
    table = meta_in[...]
    slots = []
    for row in (0, 2):
        hot = [(names == table[row + k : row + k + 1, :]).astype(F32) for k in range(2)]
        earlier = nn((hot[0] + hot[1]).astype(BF16), before)
        for k in range(2):
            place = jnp.sum(hot[k] * earlier, axis=0, keepdims=True)
            slots.append(table[row + k : row + k + 1, :] * float(CAP) + place)
    meta[z] = jnp.concatenate([*slots, table[4:8, :]], axis=0)

    partners = 2 + PLANES - 1 + 2 * (PEERS - 1)
    pl.semaphore_wait(barrier, jnp.where(jnp.logical_and(crossing, is_end), partners + 1, partners))

    def relay(t, to, stops, stop):
        source = grads_in if t == GRAD else acts_in
        number = 0 if t == GRAD else 1
        target, sem = (held, held_sem) if stop else (gath.at[t], gath_sem.at[t])
        return remote(source.at[0], target.at[z], rl_sem.at[number], sem.at[z], (to, me))

    for t, to, stops in ((GRAD, behind, first), (FWD, ahead, last)):
        pl.when(stops)(lambda: relay(t, to, stops, True).start())
        pl.when(jnp.logical_not(stops))(lambda: relay(t, to, stops, False).start())
    for k in range(1, PLANES):
        remote(meta.at[z], meta.at[z], ms_sem.at[k - 1], meta_sem.at[z], at_plane(lax.rem(z + k, PLANES))).start()

    def pass_on(t, b, right):
        return remote(
            gath.at[t, b],
            gath.at[t, b],
            zs_sem.at[t, b, 0 if right else 1],
            gath_sem.at[t, b],
            at_plane(z + 1 if right else z - 1),
        )

    def goes(t, b, right, own):
        if right:
            far, near, inner = b >= 2, (b <= z if own else b < z), z < 2
            last_hop = jnp.logical_and(z == 2, b == 3)
        else:
            far, near, inner = b < 2, (b >= z if own else b > z), z > 1
            last_hop = jnp.logical_and(z == 1, b == 0)
        hot = jnp.logical_and(crosses(t), jnp.logical_and(far, jnp.logical_or(inner, last_hop)))
        usual = jnp.logical_and(jnp.logical_not(crosses(t)), jnp.logical_and(near, inner))
        return jnp.logical_or(hot, usual)

    def take(t, b):
        wait_for(gath.at[t, b], gath_sem.at[t, b])
        for right in (True, False):
            pl.when(goes(t, b, right, False))(lambda: pass_on(t, b, right).start())

    def own(t):
        pl.when(z < 2)(lambda: pass_on(t, z, True).start())
        pl.when(z >= 2)(lambda: pass_on(t, z, False).start())

    def held_on(b, k):
        return remote(held.at[b], held.at[b], ac_sem.at[k], held_sem.at[b], at_plane(jnp.where(flip, z + 1, z - 1)))

    def held_across(b, k):
        t = jnp.where(first, FWD, GRAD)
        return remote(held.at[b], gath.at[t, b], ac_sem.at[k], gath_sem.at[t, b], across)

    def send_held(k):
        b = jnp.where(k == 0, z, jnp.where(flip, 2, 1))
        wait_for(held.at[b], held_sem.at[b])
        pl.when(is_end)(lambda: held_across(b, k).start())
        pl.when(is_mid)(lambda: held_on(b, k).start())

    def sort_rows(t, b, plane, target):
        info = meta[b]
        wanted = (lax.broadcasted_iota(jnp.int32, (PEERS * CAP, TOK), 0) + plane * (PEERS * CAP)).astype(F32)
        forward = t == FWD
        picks = [
            (wanted == jnp.where(forward, info[k : k + 1, :], info[2 + k : 3 + k, :])).astype(F32) for k in range(2)
        ]
        pick = (picks[0] + picks[1]).astype(BF16)
        gate = jnp.sum(picks[0] * info[6:7, :] + picks[1] * info[7:8, :], axis=1, keepdims=True)
        gate = jnp.where(t == GRAD, gate, 1.0)
        for c in range(0, D, 512):
            target[t, b, :, c : c + 512] = (nn(pick, gath[t, b, :, c : c + 512]) * gate).astype(BF16)

    def pack(t, b):
        sort_rows(t, b, z, pk)
        for k in range(1, PEERS):
            peer = lax.rem(lane + k, PEERS)
            remote(
                pk.at[t, b, rows(peer)], rx.at[t, b, rows(lane)], pks_sem.at[t, b], rx_sem.at[t, b], at_peer(peer)
            ).start()
        pltpu.make_async_copy(pk.at[t, b, rows(lane)], rx.at[t, b, rows(lane)], rx_sem.at[t, b]).start()

    outer = jnp.where(flip, 3, 0)
    inner = jnp.where(flip, 2, 1)

    def pack_out(t, b):
        sort_rows(t, b, outer, pk_out)
        for k in range(PEERS):
            peer = lax.rem(lane + k, PEERS)
            remote(
                pk_out.at[t, b, rows(peer)], rx.at[t, b, rows(lane)], pko_sem.at[t, b], rx_sem.at[t, b],
                (sec, outer * PEERS + peer),
            ).start()

    def give_back(x, b):
        for k in range(1, PEERS):
            peer = lax.rem(lane + k, PEERS)
            remote(
                ou.at[x, b, rows(peer)], rt.at[x, b, rows(lane)], os_sem.at[x, b], rt_sem.at[x, b], at_peer(peer)
            ).start()
        pltpu.make_async_copy(ou.at[x, b, rows(lane)], rt.at[x, b, rows(lane)], rt_sem.at[x, b]).start()

    def compute_forward(b):
        wait_for(rx.at[FWD, b], rx_sem.at[FWD, b])

        @pl.loop(0, FF // 256)
        def _(i):
            c = pl.multiple_of(i * 256, 256)
            x = rx[FWD, b]
            g = nn(x, w_in[:, pl.ds(c, 256)])
            u = nn(x, w_in[:, pl.ds(FF + c, 256)])
            hid[:, pl.ds(c, 256)] = (g * jax.nn.sigmoid(g) * u).astype(BF16)

        @pl.loop(0, D // 512)
        def _(i):
            c = pl.multiple_of(i * 512, 512)
            ou[FWD_OUT, b, :, pl.ds(c, 512)] = nn(hid[...], w_down[:, pl.ds(c, 512)]).astype(BF16)

        give_back(FWD_OUT, b)

    def compute_backward(b):
        wait_for(rx.at[SAVED, b], rx_sem.at[SAVED, b])
        wait_for(rx.at[GRAD, b], rx_sem.at[GRAD, b])

        @pl.loop(0, FF // 256)
        def _(i):
            c = pl.multiple_of(i * 256, 256)
            x = rx[SAVED, b]
            g = nn(x, w_in[:, pl.ds(c, 256)])
            u = nn(x, w_in[:, pl.ds(FF + c, 256)])
            h = nt(rx[GRAD, b], w_down[pl.ds(c, 256), :])
            s = jax.nn.sigmoid(g)
            joined[:, pl.ds(c, 256)] = (h * u * s * (1.0 + g * (1.0 - s))).astype(BF16)
            joined[:, pl.ds(FF + c, 256)] = (h * g * s).astype(BF16)

        @pl.loop(0, D // 256)
        def _(i):
            c = pl.multiple_of(i * 256, 256)
            ou[BWD_OUT, b, :, pl.ds(c, 256)] = nt(joined[...], w_in[pl.ds(c, 256), :]).astype(BF16)

        give_back(BWD_OUT, b)

    def weights_of(x, b):
        info = meta_t[b]
        wanted = (lax.broadcasted_iota(jnp.int32, (TOK, PEERS * CAP), 1) + z * (PEERS * CAP)).astype(F32)
        first = 0 if x == FWD_OUT else 2
        picks = [(wanted == info[:, first + k : first + k + 1]).astype(F32) for k in range(2)]
        if x == BWD_OUT:
            return [(picks[0] + picks[1]).astype(BF16)]
        full = picks[0] * info[:, 4:5] + picks[1] * info[:, 5:6]
        high = full.astype(BF16)
        return [high, (full - high.astype(F32)).astype(BF16)]

    def summed(x, b, weights, c):
        value = rt[x, b, :, c : c + 512]
        total = nn(weights[0], value)
        for w in weights[1:]:
            total = total + nn(w, value)
        return total

    def chain_out(x, b):
        right = b > z
        plane = jnp.where(right, z + 1, z - 1)
        slot = jnp.where(jnp.logical_and(jnp.logical_not(right), plane == b), 4, b)
        return remote(ps.at[x, b], cin.at[x, slot], ps_sem.at[x, b], cin_sem.at[x, slot], at_plane(plane))

    def reduce_step(x, b):
        wait_for(rt.at[x, b], rt_sem.at[x, b])
        weights = weights_of(x, b)
        has = is_mid

        @pl.when(has)
        def _():
            wait_for(cin.at[x, b], cin_sem.at[x, b])
            for c in range(0, D, 512):
                ps[x, b, :, c : c + 512] = (
                    summed(x, b, weights, c) + cin[x, b, :, c : c + 512].astype(F32)
                ).astype(BF16)

        @pl.when(jnp.logical_not(has))
        def _():
            for c in range(0, D, 512):
                ps[x, b, :, c : c + 512] = summed(x, b, weights, c).astype(BF16)

        chain_out(x, b).start()

    def finish(x):
        out = out_b if x == BWD_OUT else out_f
        t = GRAD if x == BWD_OUT else FWD
        wait_for(rt.at[x, z], rt_sem.at[x, z])
        weights = weights_of(x, z)

        @pl.when(z > 0)
        def _():
            wait_for(cin.at[x, z], cin_sem.at[x, z])

        @pl.when(z < 3)
        def _():
            wait_for(cin.at[x, 4], cin_sem.at[x, 4])

        for c in range(0, D, 512):
            total = gath[t, z, :, c : c + 512].astype(F32) + summed(x, z, weights, c)
            left = jnp.where(z > 0, cin[x, z, :, c : c + 512].astype(F32), 0.0)
            right = jnp.where(z < 3, cin[x, 4, :, c : c + 512].astype(F32), 0.0)
            out[0, :, c : c + 512] = (total + left + right).astype(BF16)

    def every_meta():
        for k in range(1, PLANES):
            b = lax.rem(z + k, PLANES)
            wait_for(meta.at[b], meta_sem.at[b])
        for b in range(PLANES):
            meta_t[b] = jnp.concatenate([meta[b]] * (TOK // 8), axis=0).T
        load_in.wait()
        load_down.wait()

    end_tables = [(first, END_FIRST), (last, END_LAST), (None, END_INNER)]
    mid_tables = [(first, MID_FIRST), (last, MID_LAST), (None, MID_INNER)]
    choices = [(jnp.logical_and(is_mid, c) if c is not None else is_mid, steps) for c, steps in mid_tables]
    choices += end_tables

    def seen(raw):
        return jnp.where(flip, 3 - raw, raw)

    @pl.loop(0, max(len(steps) for _, steps in choices))
    def _(i):
        code = lookup(i, choices)

        def during(start, end, run):
            pl.when(jnp.logical_and(code >= start, code < end))(lambda: run(code - start))

        during(TAKE, PACK, lambda n: take(n // 4, seen(lax.rem(n, 4))))
        during(PACK, PACK_OUT, lambda n: pack(n // 4, seen(lax.rem(n, 4))))
        during(PACK_OUT, OWN, lambda n: pack_out(n // 4, seen(lax.rem(n, 4))))
        during(OWN, MAKE_B, own)
        during(MAKE_B, MAKE_F, lambda n: compute_backward(seen(n)))
        during(MAKE_F, SUM_B, lambda n: compute_forward(seen(n)))
        during(SUM_B, SUM_F, lambda n: reduce_step(BWD_OUT, seen(n)))
        during(SUM_F, FINISH, lambda n: reduce_step(FWD_OUT, seen(n)))
        during(FINISH, FINISH + 1, lambda n: finish(BWD_OUT))
        during(FINISH + 1, TABLES, lambda n: finish(FWD_OUT))
        during(TABLES, ACROSS, lambda n: every_meta())
        during(ACROSS, LAST, send_held)

    wait_for(held.at[z], rl_sem.at[0])
    wait_for(held.at[z], rl_sem.at[1])
    pl.when(crossing)(lambda: wait_for(held.at[z], ac_sem.at[0]))
    pl.when(jnp.logical_and(crossing, is_end))(lambda: wait_for(held.at[z], ac_sem.at[1]))
    for k in range(1, PLANES):
        remote(meta.at[z], meta.at[z], ms_sem.at[k - 1], meta_sem.at[z], at_plane(lax.rem(z + k, PLANES))).wait_send()
    sent = pl.ds(0, (PEERS - 1) * CAP)
    for b in range(PLANES):
        for t in range(3):
            for right in (True, False):
                pl.when(goes(t, b, right, True))(lambda: pass_on(t, b, right).wait_send())

            whole = jnp.logical_or(jnp.logical_and(crosses(t), b != inner), jnp.logical_and(jnp.logical_not(crosses(t)), b == outer))
            pl.when(jnp.logical_or(is_mid, whole))(lambda: wait_for(pk.at[t, b, sent], pks_sem.at[t, b]))

            usual = jnp.logical_and(jnp.logical_not(crosses(t)), b != outer)
            hot = jnp.logical_and(crosses(t), b == inner)
            pl.when(jnp.logical_and(is_mid, jnp.logical_or(usual, hot)))(
                lambda: wait_for(pk_out.at[t, b], pko_sem.at[t, b])
            )
        for x in range(2):
            wait_for(ou.at[x, b, sent], os_sem.at[x, b])
            pl.when(b != z)(lambda: wait_for(ps.at[x, b], ps_sem.at[x, b]))


def per_device(acts, f_routes, f_gates, w_in, w_down, saved, b_routes, b_gates, grads):
    table = jnp.concatenate(
        [f_routes[0].T.astype(F32), b_routes[0].T.astype(F32), f_gates[0].T, b_gates[0].T], axis=0
    )
    dma = pltpu.SemaphoreType.DMA
    block = (TOK, D)
    out = jax.ShapeDtypeStruct((1, TOK, D), BF16)
    vmem = pl.BlockSpec(memory_space=pltpu.VMEM)
    hbm = pl.BlockSpec(memory_space=pl.ANY)
    return tuple(
        pl.pallas_call(
            kernel,
            name="moe_relay",
            out_shape=(out, out),
            in_specs=[vmem, hbm, hbm, hbm, hbm, hbm],
            out_specs=(vmem, vmem),
            scratch_shapes=[
                pltpu.VMEM((3, PLANES, *block), BF16),
                pltpu.VMEM((PLANES, *block), BF16),
                pltpu.VMEM((3, PLANES, *block), BF16),
                pltpu.VMEM((3, PLANES, *block), BF16),
                pltpu.VMEM((3, PLANES, *block), BF16),
                pltpu.VMEM((2, PLANES, *block), BF16),
                pltpu.VMEM((2, PLANES, *block), BF16),
                pltpu.VMEM((2, PLANES + 1, *block), BF16),
                pltpu.VMEM((2, PLANES, *block), BF16),
                pltpu.VMEM((D, 2 * FF), BF16),
                pltpu.VMEM((FF, D), BF16),
                pltpu.VMEM((TOK, FF), BF16),
                pltpu.VMEM((TOK, 2 * FF), BF16),
                pltpu.VMEM((PLANES, 8, TOK), F32),
                pltpu.VMEM((PLANES, TOK, TOK), F32),
                dma((3, PLANES)),
                dma((PLANES,)),
                dma((2,)),
                dma((3, PLANES, 2)),
                dma((3, PLANES)),
                dma((3, PLANES)),
                dma((3, PLANES)),
                dma((2, PLANES)),
                dma((2, PLANES)),
                dma((2, PLANES + 1)),
                dma((2, PLANES)),
                dma((PLANES,)),
                dma((PLANES - 1,)),
                dma((2,)),
                dma((2,)),
            ],
            compiler_params=pltpu.CompilerParams(
                collective_id=0, has_side_effects=True, vmem_limit_bytes=62 * 2**20
            ),
        )(table, acts, saved, grads, w_in, w_down)
    )


def solution(mesh):
    rows = P("section", "expert", None)
    weights = P("section", "expert", None, None)
    return jax.shard_map(
        per_device,
        mesh=mesh,
        in_specs=(rows, rows, rows, weights, weights, rows, rows, rows, rows),
        out_specs=(rows, rows),
        check_vma=False,
    )
```
